512 devices in a mesh: dp: 8 (over y, x_hi), ctx: 32 (over z, core), mp: 2 (over x_lo).
Axes of the slice: x: 4 (x_hi: 2, x_lo: 2; x = x_hi * 2 + x_lo), y: 4, z: 16, core: 2. Of those that a mesh axis runs over, the one named last changes fastest.
Arguments:
- query_input: bfloat16 [8, 14336, 1024], P('dp', 'ctx', 'mp'), may hold values from -6 to 6
- key_input: bfloat16 [8, 14336, 1024], P('dp', 'ctx', 'mp'), may hold values from -6 to 6
- value_input: bfloat16 [8, 14336, 1024], P('dp', 'ctx', 'mp'), may hold values from -6 to 6
- taps: float32 [3, 3, 1024], P(None, None, 'mp'), may hold values from -1.5 to 1.5
- grad_out: bfloat16 [8, 14336, 1024], P('dp', 'ctx', 'mp'), may hold values from -6 to 6
Outputs:
- attn_out: bfloat16 [8, 14336, 1024], P('dp', 'ctx', 'mp')
- grad_q: bfloat16 [8, 14336, 1024], P('dp', 'ctx', 'mp')
- grad_k: bfloat16 [8, 14336, 1024], P('dp', 'ctx', 'mp')
- value_input_gradient: bfloat16 [8, 14336, 1024], P('dp', 'ctx', 'mp')
- grad_taps: float32 [3, 3, 1024], P(None, None, 'mp')
The draws below stay inside these ranges and needn't reach their ends.
All inputs are finite; a program needn't handle non-finite values.
Results may differ from the reference program's by a relative error of at most 0.0034.
The reference program's roundings to bfloat16 on the way count: a program that leaves them out, or rounds other values in their place, can miss the bound.
Values may be sent and summed in bfloat16 or wider, within the bound.
A program may use at most 64 MiB of HBM per device.

```python
import jax
import jax.numpy as jnp
from jax import lax

HEAD_DIM = 128
STEPS = 3
TOK_DEV = 448
FEATS = 1024
SEQS = 8
LENGTH = 14336
N_CTX = 32


def draw_query_input(key, part):
    key = jax.random.fold_in(key, 11)
    return jnp.clip(jax.random.normal(key, (SEQS, LENGTH, FEATS), jnp.float32), -6.0, 6.0).astype(jnp.bfloat16)


def draw_key_input(key, part):
    key = jax.random.fold_in(key, 12)
    return jnp.clip(jax.random.normal(key, (SEQS, LENGTH, FEATS), jnp.float32), -6.0, 6.0).astype(jnp.bfloat16)


def draw_taps(key, part):
    key = jax.random.fold_in(key, 13)
    first_key = jax.random.fold_in(key, 1)
    other_key = jax.random.fold_in(key, 2)
    first_tap = jax.random.uniform(first_key, (3, 1, FEATS), jnp.float32, 0.6, 1.4)
    other_taps = jnp.clip(0.5 * jax.random.normal(other_key, (3, 2, FEATS), jnp.float32), -1.5, 1.5)
    return jnp.concatenate([first_tap, other_taps], 1)


def shard_levels(own_key, dims, shards, smallest, top_value):
    factor_of, own = 1.0, jax.random.fold_in(own_key, 6)
    for axis_at, blocks in shards:
        steps = jnp.exp(jax.random.uniform(jax.random.fold_in(own, axis_at), (blocks,), jnp.float32, smallest / len(shards), top_value / len(shards)))
        factor_of = factor_of * jnp.repeat(steps, dims[axis_at] // blocks).reshape([-1 if axis == axis_at else 1 for axis in range(len(dims))])
    return factor_of


def noise(rng, dims, width, limit, pieces=(), kind=jnp.bfloat16):
    factor_of = shard_levels(rng, dims, pieces, -0.22, 0.18) if pieces else 1.0
    result = jax.random.normal(rng, dims, jnp.float32) * width * factor_of
    return jnp.minimum(jnp.maximum(result, -limit), limit).astype(kind)


def setup_inputs(seed: int = 0) -> dict:
    key_of = jax.random.split(jax.random.key(seed), 6)
    query_input = draw_query_input(jax.random.fold_in(key_of[5], 71), 0)
    key_input = draw_key_input(jax.random.fold_in(key_of[5], 71), 0)
    value_input = noise(key_of[2], (SEQS, LENGTH, FEATS), 1.0, 6.0, ((0, 8), (1, 32), (2, 2)))
    taps = draw_taps(jax.random.fold_in(key_of[5], 71), 0)
    grad_out = noise(key_of[4], (SEQS, LENGTH, FEATS), 1.0, 6.0, ((0, 8), (1, 32), (2, 2)))
    return dict(query_input=query_input, key_input=key_input, value_input=value_input, taps=taps, grad_out=grad_out)


def featurize(unfiltered_input, tap):
    total = jnp.zeros(unfiltered_input.shape, jnp.float32)
    for j in range(3):
        total = total + tap[j] * jnp.roll(unfiltered_input, j, axis=1).astype(jnp.float32)
    return total.astype(jnp.bfloat16)


def featurizer_adjoint(feature_gradient, tap):
    total = jnp.zeros(feature_gradient.shape, jnp.float32)
    for j in range(3):
        total = total + tap[j] * jnp.roll(feature_gradient, -j, axis=1).astype(jnp.float32)
    return total.astype(jnp.bfloat16)


def reference(query_input, key_input, value_input, taps, grad_out):
    sequence_count, length_total, feature_maps = query_input.shape
    nblocks = N_CTX
    block = TOK_DEV
    heads = feature_maps // HEAD_DIM
    scale = HEAD_DIM ** -0.5
    qf = featurize(query_input, taps[0])
    kf = featurize(key_input, taps[1])
    vf = featurize(value_input, taps[2])
    shape = (sequence_count, nblocks, block, heads, HEAD_DIM)
    q_blocks = qf.reshape(shape)
    k_blocks = kf.reshape(shape)
    v_blocks = vf.reshape(shape)
    g_blocks = grad_out.reshape(shape)
    causal = jnp.arange(block)[None, :] <= jnp.arange(block)[:, None]

    def take(arr, index):
        return lax.dynamic_index_in_dim(arr, index, 1, keepdims=False)

    def step(carry, bidx):
        dk_acc, value_gradient_total = carry
        qblk = take(q_blocks, bidx).astype(jnp.float32)
        gblk = take(g_blocks, bidx).astype(jnp.float32)
        where = [((bidx - s) % nblocks).astype(jnp.int32) for s in range(STEPS + 1)]
        kblks = [take(k_blocks, w).astype(jnp.float32) for w in where]
        vblks = [take(v_blocks, w).astype(jnp.float32) for w in where]
        scores = []
        for s in range(STEPS + 1):
            sc = jnp.einsum("sqhd,skhd->shqk", qblk, kblks[s]) * scale
            if s == 0:
                sc = jnp.where(causal, sc, -jnp.inf)
            scores.append(sc)
        peak = jnp.max(jnp.stack([sc.max(-1) for sc in scores]), axis=0)
        total = sum(jnp.exp(sc - peak[..., None]).sum(-1) for sc in scores)
        lse = peak + jnp.log(total)
        probs = [jnp.exp(sc - lse[..., None]) for sc in scores]
        pbfs = [lax.optimization_barrier(p.astype(jnp.bfloat16)).astype(jnp.float32) for p in probs]
        out = sum(jnp.einsum("shqk,skhd->sqhd", pbfs[s], vblks[s]) for s in range(STEPS + 1))
        dprobs = [jnp.einsum("sqhd,skhd->shqk", gblk, vblks[s]) for s in range(STEPS + 1)]
        delta = sum((probs[s] * dprobs[s]).sum(-1) for s in range(STEPS + 1))
        dq = jnp.zeros(qblk.shape, jnp.float32)
        for s in range(STEPS + 1):
            dsc = probs[s] * (dprobs[s] - delta[..., None])
            dsc = lax.optimization_barrier(dsc.astype(jnp.bfloat16)).astype(jnp.float32)
            dq = dq + scale * jnp.einsum("shqk,skhd->sqhd", dsc, kblks[s])
            dk_term = scale * jnp.einsum("shqk,sqhd->skhd", dsc, qblk)
            dv_term = jnp.einsum("shqk,sqhd->skhd", pbfs[s], gblk)
            dk_acc = lax.dynamic_update_index_in_dim(dk_acc, take(dk_acc, where[s]) + dk_term, where[s], 1)
            value_gradient_total = lax.dynamic_update_index_in_dim(value_gradient_total, take(value_gradient_total, where[s]) + dv_term, where[s], 1)
        return (dk_acc, value_gradient_total), (out.astype(jnp.bfloat16), dq.astype(jnp.bfloat16))

    zeros = jnp.zeros(shape, jnp.float32)
    (dk_acc, value_gradient_total), (outs, dqs) = lax.scan(step, (zeros, zeros), jnp.arange(nblocks).astype(jnp.int32))
    attn_out = jnp.transpose(outs, (1, 0, 2, 3, 4)).reshape(sequence_count, length_total, feature_maps)
    query_feature_gradient = jnp.transpose(dqs, (1, 0, 2, 3, 4)).reshape(sequence_count, length_total, feature_maps)
    key_feature_gradient = dk_acc.reshape(sequence_count, length_total, feature_maps).astype(jnp.bfloat16)
    value_feature_gradient = value_gradient_total.reshape(sequence_count, length_total, feature_maps).astype(jnp.bfloat16)
    grad_q = featurizer_adjoint(query_feature_gradient, taps[0])
    grad_k = featurizer_adjoint(key_feature_gradient, taps[1])
    value_input_gradient = featurizer_adjoint(value_feature_gradient, taps[2])
    rows = []
    for unfiltered_input, feature_gradient in ((query_input, query_feature_gradient), (key_input, key_feature_gradient), (value_input, value_feature_gradient)):
        rows.append(jnp.stack([jnp.sum(feature_gradient.astype(jnp.float32) * jnp.roll(unfiltered_input, j, axis=1).astype(jnp.float32), axis=(0, 1)) for j in range(3)]))
    grad_taps = jnp.stack(rows)
    return attn_out, grad_q, grad_k, value_input_gradient, grad_taps
```

```python
import functools

import jax
import jax.numpy as jnp
from jax import lax
from jax.experimental import pallas as pl
from jax.experimental.pallas import tpu as pltpu
from jax.sharding import PartitionSpec as P

HEAD_DIM = 128
STEPS = 3
BLOCKS = STEPS + 1
RIM = 16
MESH = pl.DeviceIdType.MESH
BF16 = jnp.bfloat16
F32 = jnp.float32
NT = (((1,), (1,)), ((), ()))
NN = (((1,), (0,)), ((), ()))
TN = (((0,), (0,)), ((), ()))


def dot(a, b, dims):
    return lax.dot_general(a, b, dims, preferred_element_type=F32)


def reduction_rounds(dp, ctx):
    if (dp, ctx) == (8, 32):
        return (
            (("ctx", 1, 2), ("dp", 1, 2)),
            (("dp", 2, 4),),
            (("ctx", 2, 4),),
            (("ctx", 8, 4),),
        )
    return tuple(((name, 1, size),) for name, size in (("dp", dp), ("ctx", ctx)) if size > 1)


class Group:
    def __init__(self, digits, place):
        self.digits = digits
        self.place = place
        self.size = 1
        self.index = 0
        for name, stride, size in digits:
            self.index = self.index * size + (place[name] // stride) % size
            self.size *= size

    def other(self, ahead):
        slot = lax.rem(self.index + ahead, self.size)
        rest = slot
        device = {}
        for name, stride, size in reversed(self.digits):
            digit = lax.rem(rest, size)
            rest = rest // size
            mine = (self.place[name] // stride) % size
            device[name] = self.place[name] + (digit - mine) * stride
        return slot, device


def kernel(
    sizes, q_hbm, k_hbm, v_hbm, taps_ref, g_hbm,
    out_hbm, gq_hbm, gk_hbm, gv_hbm, gt_ref,
    raw, qraw, gbuf, ext, qext, kfb, vfb, qfb, pbuf, dsbuf, dkv, dqb,
    rf32, rb16, sb16, tail_out, tail_in, dext, obuf, abuf, total, slots,
    in_sem, out_sem, attn_sem, rim_send, rim_recv, fwd_send, fwd_recv, bwd_send, bwd_recv,
    tail_send, tail_recv, sum_send, sum_recv,
):
    rows, heads, n_dp, n_ctx = sizes
    nkeys = BLOCKS * rows
    split = (nkeys - rows) // 128 * 128
    offset = nkeys - rows - split
    tile = rows // 2
    chunk = rows // 4
    scale = HEAD_DIM ** (-0.5)
    exp_scale = scale * 1.4426950408889634

    me = lax.axis_index("ctx")
    place = {"ctx": me, "dp": lax.axis_index("dp")}
    core = lax.rem(me, 2)
    ahead = {"ctx": lax.rem(me + 1, n_ctx)}
    behind = {"ctx": lax.rem(me + n_ctx - 1, n_ctx)}
    far_ahead = {"ctx": lax.rem(me + BLOCKS, n_ctx)}
    far_behind = {"ctx": lax.rem(me + n_ctx - BLOCKS, n_ctx)}
    groups = [Group(digits, place) for digits in reduction_rounds(n_dp, n_ctx)]

    def columns(h):
        return pl.ds(h * HEAD_DIM, HEAD_DIM)

    def load(h, n):
        source = (k_hbm, v_hbm, q_hbm, g_hbm)[n].at[:, columns(h)]
        if n < 2:
            target = raw.at[h, n, pl.ds(RIM + STEPS * rows, rows), :]
        elif n == 2:
            target = qraw.at[h, pl.ds(RIM, rows), :]
        else:
            target = gbuf.at[h]
        return pltpu.make_async_copy(source, target, in_sem.at[h, n])

    for h in range(heads):
        for n in range(4):
            load(h, n).start()

    barrier = pltpu.get_barrier_semaphore()
    partners = [ahead, behind, far_ahead, far_behind]
    for group in groups:
        for m in range(1, group.size):
            partners.append(group.other(m)[1])
    for partner in partners:
        pl.semaphore_signal(barrier, inc=1, device_id=partner, device_id_type=MESH)
    pl.semaphore_wait(barrier, len(partners))

    for h in range(heads):
        for n in range(4):
            load(h, n).wait()

    def pass_on(step, h, a):
        return pltpu.make_async_remote_copy(
            src_ref=raw.at[h, a, pl.ds(RIM + (STEPS - step) * rows, rows), :],
            dst_ref=raw.at[h, a, pl.ds(RIM + (STEPS - 1 - step) * rows, rows), :],
            send_sem=fwd_send.at[step, h, a],
            recv_sem=fwd_recv.at[step, h, a],
            device_id=ahead,
            device_id_type=MESH,
        )

    def send_step(step, h):
        for a in range(2):
            if step > 0:
                pass_on(step - 1, h, a).wait_recv()
            pass_on(step, h, a).start()

    q_rim = pltpu.make_async_remote_copy(
        src_ref=qraw.at[:, pl.ds(rows, RIM), :],
        dst_ref=qraw.at[:, pl.ds(0, RIM), :],
        send_sem=rim_send.at[0],
        recv_sem=rim_recv.at[0],
        device_id=ahead,
        device_id_type=MESH,
    )
    kv_rim = pltpu.make_async_remote_copy(
        src_ref=raw.at[:, :, pl.ds(nkeys, RIM), :],
        dst_ref=raw.at[:, :, pl.ds(0, RIM), :],
        send_sem=rim_send.at[1],
        recv_sem=rim_recv.at[1],
        device_id=far_ahead,
        device_id_type=MESH,
    )

    send_step(0, 0)
    q_rim.start()
    kv_rim.start()
    total[...] = jnp.zeros_like(total)
    send_step(1, 0)
    send_step(2, 0)
    if heads > 1:
        send_step(0, 1)
    q_rim.wait_recv()
    kv_rim.wait_recv()

    def bwd_narrow(step, h, a):
        return pltpu.make_async_remote_copy(
            src_ref=sb16.at[h, step, a],
            dst_ref=rb16.at[h, step, a],
            send_sem=bwd_send.at[step, h, a],
            recv_sem=bwd_recv.at[step, h, a],
            device_id=behind,
            device_id_type=MESH,
        )

    def bwd_wide(step, h, a):
        return pltpu.make_async_remote_copy(
            src_ref=dkv.at[h, a, pl.ds(step * rows, rows), :],
            dst_ref=rf32.at[h, step, a],
            send_sem=bwd_send.at[step, h, a],
            recv_sem=bwd_recv.at[step, h, a],
            device_id=behind,
            device_id_type=MESH,
        )

    def send_back(step, h):
        @pl.when(core == 0)
        def _():
            for a in range(2):
                if step > 0:
                    bwd_wide(step - 1, h, a).wait_recv()

                def piece(i, carry):
                    at = pl.multiple_of(i * chunk, 16)
                    term = dkv[h, a, pl.ds(step * rows + at, chunk), :]
                    if step > 0:
                        term = term + rf32[h, step - 1, a, pl.ds(at, chunk), :]
                    sb16[h, step, a, pl.ds(at, chunk), :] = term.astype(BF16)
                    return carry

                lax.fori_loop(0, rows // chunk, piece, 0)
                bwd_narrow(step, h, a).start()

        @pl.when(core == 1)
        def _():
            for a in range(2):
                if step > 0:
                    bwd_narrow(step - 1, h, a).wait_recv()

                    def piece(i, carry):
                        at = pl.multiple_of(i * chunk, 16)
                        here = pl.ds(step * rows + at, chunk)
                        came = rb16[h, step - 1, a, pl.ds(at, chunk), :].astype(F32)
                        dkv[h, a, here, :] = dkv[h, a, here, :] + came
                        return carry

                    lax.fori_loop(0, rows // chunk, piece, 0)
                bwd_wide(step, h, a).start()

    def tail(h):
        return pltpu.make_async_remote_copy(
            src_ref=tail_out.at[h],
            dst_ref=tail_in.at[h],
            send_sem=tail_send.at[h],
            recv_sem=tail_recv.at[h],
            device_id=behind,
            device_id_type=MESH,
        )

    def settle(h):
        last = STEPS - 1

        @pl.when(core == 0)
        def _():
            for a in range(2):
                bwd_wide(last, h, a).wait_recv()

        @pl.when(core == 1)
        def _():
            for a in range(2):
                bwd_narrow(last, h, a).wait_recv()

        def piece(i, carry):
            at = pl.multiple_of(i * chunk, 16)
            here = pl.ds(at, chunk)
            dext[0, here, :] = dqb[h, here, :].astype(F32)
            for a in range(2):
                own = dkv[h, a, pl.ds(STEPS * rows + at, chunk), :]

                @pl.when(core == 0)
                def _():
                    dext[a + 1, here, :] = (own + rf32[h, last, a, here, :]).astype(BF16).astype(F32)

                @pl.when(core == 1)
                def _():
                    came = rb16[h, last, a, here, :].astype(F32)
                    dext[a + 1, here, :] = (own + came).astype(BF16).astype(F32)

            return carry

        lax.fori_loop(0, rows // chunk, piece, 0)
        for a in range(3):
            tail_out[h, a] = dext[a, pl.ds(0, RIM), :].astype(BF16)
        tail(h).start()

    def tap(a, j, h):
        return taps_ref[a, pl.ds(j, 1), columns(h)]

    def store(h, a):
        target = (gq_hbm, gk_hbm, gv_hbm)[a]
        return pltpu.make_async_copy(obuf.at[h, a], target.at[:, columns(h)], out_sem.at[h, a])

    def finish(h):
        tail(h).wait_recv()
        for a in range(3):
            dext[a, pl.ds(rows, RIM), :] = tail_in[h, a].astype(F32)
            taps_here = [tap(a, j, h) for j in range(3)]
            for i in range(rows // chunk):
                value = jnp.zeros((chunk, HEAD_DIM), F32)
                for j in range(3):
                    value = value + taps_here[j] * dext[a, pl.ds(i * chunk + j, chunk), :]
                obuf[h, a, pl.ds(i * chunk, chunk), :] = value.astype(BF16)
            store(h, a).start()

    def featurize(h):
        for a, (source, wide, target, blocks) in enumerate(
            (
                (qraw.at[h], qext, qfb, 1),
                (raw.at[h, 0], ext.at[0], kfb, BLOCKS),
                (raw.at[h, 1], ext.at[1], vfb, BLOCKS),
            )
        ):
            taps_here = [tap(a, j, h) for j in range(3)]
            wide[pl.ds(0, RIM), :] = source[pl.ds(0, RIM), :].astype(F32)
            for i in range(blocks * rows // chunk):
                here = pl.ds(RIM + i * chunk, chunk)
                wide[here, :] = source[here, :].astype(F32)
                value = jnp.zeros((chunk, HEAD_DIM), F32)
                for j in range(3):
                    value = value + taps_here[j] * wide[pl.ds(RIM + i * chunk - j, chunk), :]
                target[pl.ds(i * chunk, chunk), :] = value.astype(BF16)

    def attend(h, i):
        here = pl.ds(i * tile, tile)
        q = qfb[here, :]
        g = gbuf[h, here, :]
        parts = (pl.ds(0, split), pl.ds(split, nkeys - split))
        scores = [dot(q, kfb[part, :], NT) for part in parts]
        row = lax.broadcasted_iota(jnp.int32, scores[1].shape, 0) + i * tile
        col = lax.broadcasted_iota(jnp.int32, scores[1].shape, 1) - offset
        scores[1] = jnp.where(col <= row, scores[1], -jnp.inf)
        peak = jnp.maximum(
            jnp.max(scores[0], axis=1, keepdims=True), jnp.max(scores[1], axis=1, keepdims=True)
        )
        weights = [jnp.exp2((score - peak) * exp_scale) for score in scores]
        norm = jnp.sum(weights[0], axis=1, keepdims=True) + jnp.sum(weights[1], axis=1, keepdims=True)
        inverse = 1.0 / norm
        probs = [weight * inverse for weight in weights]
        attended = jnp.zeros((tile, HEAD_DIM), F32)
        for part, prob in zip(parts, probs, strict=True):
            prob_b = prob.astype(BF16)
            pbuf[here, part] = prob_b
            attended = attended + dot(prob_b, vfb[part, :], NN)
        abuf[h, here, :] = attended.astype(BF16)
        terms = [prob * dot(g, vfb[part, :], NT) for part, prob in zip(parts, probs, strict=True)]
        delta = jnp.sum(terms[0], axis=1, keepdims=True) + jnp.sum(terms[1], axis=1, keepdims=True)
        query_grad = jnp.zeros((tile, HEAD_DIM), F32)
        for part, prob, term in zip(parts, probs, terms, strict=True):
            score_grad = (term - prob * delta).astype(BF16)
            dsbuf[here, part] = score_grad
            query_grad = query_grad + dot(score_grad, kfb[part, :], NN)
        dqb[h, here, :] = (query_grad * scale).astype(BF16)

    def attn_store(h):
        return pltpu.make_async_copy(abuf.at[h], out_hbm.at[:, columns(h)], attn_sem.at[h])

    def key_gradients(h):
        attn_store(h).start()
        dkv[h, 0] = (dot(qfb[...], dsbuf[...], TN) * scale).T
        dkv[h, 1] = dot(gbuf[h], pbuf[...], TN).T
        send_back(0, h)

        def piece(i, carry):
            at = pl.multiple_of(i * chunk, 16)
            sums = list(carry)
            for a in range(2):
                term = dkv[h, a, pl.ds(at, chunk), :]
                for j in range(3):
                    near = ext[a, pl.ds(RIM - j + at, chunk), :]
                    sums[a * 3 + j] = sums[a * 3 + j] + jnp.sum(
                        (term * near).reshape(chunk // 8, 8, HEAD_DIM), axis=0
                    )
            return tuple(sums)

        sums = lax.fori_loop(
            0, nkeys // chunk, piece, tuple(jnp.zeros((8, HEAD_DIM), F32) for _ in range(6))
        )
        for j in range(3):
            query_sum = jnp.sum(
                dqb[h].astype(F32) * qext[pl.ds(RIM - j, rows), :], axis=0, keepdims=True
            )
            total[h, pl.ds(j, 1), :] = query_sum
        for n in range(6):
            total[h, pl.ds(3 + n, 1), :] = jnp.sum(sums[n], axis=0, keepdims=True)

    def head_step(h, carry):
        for a in range(2):
            pass_on(STEPS - 1, h, a).wait_recv()
        featurize(h)

        @pl.when(h < heads - 1)
        def _():
            send_step(1, h + 1)

        @pl.when(h > 1)
        def _():
            settle(h - 2)

        attend(h, 0)

        @pl.when(h < heads - 1)
        def _():
            send_step(2, h + 1)

        @pl.when(h < heads - 2)
        def _():
            send_step(0, h + 2)

        @pl.when(h > 0)
        def _():
            send_back(1, h - 1)

        @pl.when(h > 1)
        def _():
            finish(h - 2)

        attend(h, 1)

        @pl.when(h > 0)
        def _():
            send_back(2, h - 1)

        key_gradients(h)
        return carry

    lax.fori_loop(0, heads, head_step, 0)

    def sum_copy(n, m):
        group = groups[n]
        slot, device = group.other(m)
        return slot, pltpu.make_async_remote_copy(
            src_ref=slots.at[n, group.index],
            dst_ref=slots.at[n, group.index],
            send_sem=sum_send.at[n, m],
            recv_sem=sum_recv.at[n, group.index],
            device_id=device,
            device_id_type=MESH,
        )

    def sum_start(n, value):
        slots[n, groups[n].index] = value
        for m in range(1, groups[n].size):
            sum_copy(n, m)[1].start()

    def sum_end(n):
        group = groups[n]
        for m in range(1, group.size):
            slot, _ = group.other(m)
            pltpu.make_async_remote_copy(
                src_ref=slots.at[n, slot],
                dst_ref=slots.at[n, slot],
                send_sem=sum_send.at[n, m],
                recv_sem=sum_recv.at[n, slot],
                device_id=ahead,
                device_id_type=MESH,
            ).wait_recv()
        value = slots[n, 0]
        for slot in range(1, group.size):
            value = value + slots[n, slot]
        return value

    steps = []
    if heads > 1:
        steps.append(lambda: settle(heads - 2))
        steps.append(lambda: finish(heads - 2))
    steps.append(lambda: send_back(1, heads - 1))
    steps.append(lambda: send_back(2, heads - 1))
    steps.append(lambda: settle(heads - 1))
    steps.append(lambda: finish(heads - 1))

    sum_start(0, total[...])
    done = 0
    for n, step in enumerate(steps):
        step()
        if n > 0 and done < len(groups) - 1:
            sum_start(done + 1, sum_end(done))
            done += 1
    while done < len(groups) - 1:
        sum_start(done + 1, sum_end(done))
        done += 1
    value = sum_end(done)
    for h in range(heads):
        for a in range(3):
            gt_ref[a, :, columns(h)] = value[h, 3 * a : 3 * a + 3, :]

    for h in range(heads):
        attn_store(h).wait()
        tail(h).wait_send()
        for a in range(3):
            store(h, a).wait()
        for step in range(STEPS):
            for a in range(2):
                pass_on(step, h, a).wait_send()

    @pl.when(core == 0)
    def _():
        for h in range(heads):
            for step in range(STEPS):
                for a in range(2):
                    bwd_narrow(step, h, a).wait_send()

    @pl.when(core == 1)
    def _():
        for h in range(heads):
            for step in range(STEPS):
                for a in range(2):
                    bwd_wide(step, h, a).wait_send()

    q_rim.wait_send()
    kv_rim.wait_send()
    for n, group in enumerate(groups):
        for m in range(1, group.size):
            sum_copy(n, m)[1].wait_send()


def shards(n_dp, n_ctx, query_input, key_input, value_input, taps, grad_out):
    rows, width = query_input.shape[1:]
    heads = width // HEAD_DIM
    nkeys = BLOCKS * rows
    rounds = len(reduction_rounds(n_dp, n_ctx))
    members = 4 if (n_dp, n_ctx) == (8, 32) else max(n_dp, n_ctx)
    hbm = pl.BlockSpec(memory_space=pl.ANY)
    vmem = pl.BlockSpec(memory_space=pltpu.VMEM)
    flat = jax.ShapeDtypeStruct((rows, width), BF16)
    dma = pltpu.SemaphoreType.DMA
    block = (rows, HEAD_DIM)
    results = pl.pallas_call(
        functools.partial(kernel, (rows, heads, n_dp, n_ctx)),
        out_shape=(flat, flat, flat, flat, jax.ShapeDtypeStruct(taps.shape, F32)),
        in_specs=[hbm, hbm, hbm, vmem, hbm],
        out_specs=(hbm, hbm, hbm, hbm, vmem),
        scratch_shapes=[
            pltpu.VMEM((heads, 2, RIM + nkeys, HEAD_DIM), BF16),
            pltpu.VMEM((heads, RIM + rows, HEAD_DIM), BF16),
            pltpu.VMEM((heads, *block), BF16),
            pltpu.VMEM((2, RIM + nkeys, HEAD_DIM), F32),
            pltpu.VMEM((RIM + rows, HEAD_DIM), F32),
            pltpu.VMEM((nkeys, HEAD_DIM), BF16),
            pltpu.VMEM((nkeys, HEAD_DIM), BF16),
            pltpu.VMEM(block, BF16),
            pltpu.VMEM((rows, nkeys), BF16),
            pltpu.VMEM((rows, nkeys), BF16),
            pltpu.VMEM((heads, 2, nkeys, HEAD_DIM), F32),
            pltpu.VMEM((heads, *block), BF16),
            pltpu.VMEM((heads, STEPS, 2, *block), F32),
            pltpu.VMEM((heads, STEPS, 2, *block), BF16),
            pltpu.VMEM((heads, STEPS, 2, *block), BF16),
            pltpu.VMEM((heads, 3, RIM, HEAD_DIM), BF16),
            pltpu.VMEM((heads, 3, RIM, HEAD_DIM), BF16),
            pltpu.VMEM((3, rows + RIM, HEAD_DIM), F32),
            pltpu.VMEM((heads, 3, *block), BF16),
            pltpu.VMEM((heads, *block), BF16),
            pltpu.VMEM((heads, 16, HEAD_DIM), F32),
            pltpu.VMEM((rounds, members, heads, 16, HEAD_DIM), F32),
            dma((heads, 4)),
            dma((heads, 3)),
            dma((heads,)),
            dma((2,)),
            dma((2,)),
            dma((STEPS, heads, 2)),
            dma((STEPS, heads, 2)),
            dma((STEPS, heads, 2)),
            dma((STEPS, heads, 2)),
            dma((heads,)),
            dma((heads,)),
            dma((rounds, members)),
            dma((rounds, members)),
        ],
        compiler_params=pltpu.CompilerParams(
            collective_id=0, has_side_effects=True, vmem_limit_bytes=58 * 1024 * 1024
        ),
    )(query_input[0], key_input[0], value_input[0], taps, grad_out[0])
    return (*[result[None] for result in results[:4]], results[4])


def solution(mesh):
    sharded = P("dp", "ctx", "mp")
    return jax.shard_map(
        functools.partial(shards, mesh.shape["dp"], mesh.shape["ctx"]),
        mesh=mesh,
        in_specs=(sharded, sharded, sharded, P(None, None, "mp"), sharded),
        out_specs=(sharded, sharded, sharded, sharded, P(None, None, "mp")),
        check_vma=False,
    )
```

```python
import functools

import jax
import jax.numpy as jnp
from jax import lax
from jax.experimental import pallas as pl
from jax.experimental.pallas import tpu as pltpu
from jax.sharding import PartitionSpec as P

HEAD_DIM = 128
STEPS = 3
BLOCKS = STEPS + 1
RIM = 16
MESH = pl.DeviceIdType.MESH
BF16 = jnp.bfloat16
F32 = jnp.float32
NT = (((1,), (1,)), ((), ()))
NN = (((1,), (0,)), ((), ()))
TN = (((0,), (0,)), ((), ()))


def dot(a, b, dims):
    return lax.dot_general(a, b, dims, preferred_element_type=F32)


def encode(value):
    return (value * jnp.abs(value)).astype(BF16)


def decode(code):
    code = code.astype(F32)
    return code * lax.rsqrt(jnp.maximum(jnp.abs(code), 1e-37))


def reduction_rounds(dp, ctx):
    if (dp, ctx) == (8, 32):
        return (
            (("ctx", 1, 2), ("dp", 1, 2)),
            (("dp", 2, 4),),
            (("ctx", 2, 4),),
            (("ctx", 8, 4),),
        )
    return tuple(((name, 1, size),) for name, size in (("dp", dp), ("ctx", ctx)) if size > 1)


class Group:
    def __init__(self, digits, place):
        self.digits = digits
        self.place = place
        self.size = 1
        self.index = 0
        for name, stride, size in digits:
            self.index = self.index * size + (place[name] // stride) % size
            self.size *= size

    def other(self, ahead):
        slot = lax.rem(self.index + ahead, self.size)
        rest = slot
        device = {}
        for name, stride, size in reversed(self.digits):
            digit = lax.rem(rest, size)
            rest = rest // size
            mine = (self.place[name] // stride) % size
            device[name] = self.place[name] + (digit - mine) * stride
        return slot, device


def kernel(
    sizes, q_hbm, k_hbm, v_hbm, taps_ref, g_hbm,
    out_ref, gq_ref, gk_ref, gv_ref, gt_ref,
    held, mine, rim_out, near_rim, far_rim, raw, wide_own, ext, norms, kfb, vfb, qfb, sbuf, dpbuf, pbuf, dsbuf, dkv, dqb,
    term_in, term_out, tail_out, tail_in, dext, total, slots,
    in_sem, rim_send, rim_recv, fwd_send, fwd_recv, bwd_send, bwd_recv,
    tail_send, tail_recv, sum_send, sum_recv,
):
    rows, heads, n_dp, n_ctx = sizes
    nkeys = BLOCKS * rows
    past = STEPS * rows
    tile = rows // 2
    strip = min(32, tile)
    chunk = rows // 4
    scale = HEAD_DIM ** (-0.5)
    exp_scale = scale * 1.4426950408889634

    me = lax.axis_index("ctx")
    place = {"ctx": me, "dp": lax.axis_index("dp")}
    ahead = {"ctx": lax.rem(me + 1, n_ctx)}
    behind = {"ctx": lax.rem(me + n_ctx - 1, n_ctx)}
    far_ahead = {"ctx": lax.rem(me + BLOCKS, n_ctx)}
    far_behind = {"ctx": lax.rem(me + n_ctx - BLOCKS, n_ctx)}

    def width_of(i):
        return -(-(past + (i + 1) * tile) // HEAD_DIM) * HEAD_DIM

    groups = [Group(digits, place) for digits in reduction_rounds(n_dp, n_ctx)]

    def columns(h):
        return pl.ds(pl.multiple_of(h * HEAD_DIM, HEAD_DIM), HEAD_DIM)

    def load(n):
        return pltpu.make_async_copy((q_hbm, k_hbm, v_hbm, g_hbm)[n], held.at[n], in_sem.at[n])

    for n in (1, 2, 0, 3):
        load(n).start()

    barrier = pltpu.get_barrier_semaphore()
    partners = [ahead, behind, far_ahead, far_behind]
    for group in groups:
        for m in range(1, group.size):
            partners.append(group.other(m)[1])
    for partner in partners:
        pl.semaphore_signal(barrier, inc=1, device_id=partner, device_id_type=MESH)
    pl.semaphore_wait(barrier, len(partners))

    def split(h, a):
        def piece(i, carry):
            here = pl.ds(pl.multiple_of(i * chunk, 16), chunk)
            mine[h, a, here, :] = held[a + 1, here, columns(h)]
            return carry

        lax.fori_loop(0, rows // chunk, piece, 0)

    def pass_on(step, h, a):
        here = pl.ds((STEPS - step) * rows, rows)
        return pltpu.make_async_remote_copy(
            src_ref=mine.at[h, a] if step == 0 else raw.at[h, a, here, :],
            dst_ref=raw.at[h, a, pl.ds((STEPS - 1 - step) * rows, rows), :],
            send_sem=fwd_send.at[step, h, a],
            recv_sem=fwd_recv.at[step, h, a],
            device_id=ahead,
            device_id_type=MESH,
        )

    def send_step(step, h):
        for a in range(2):
            if step > 0:
                pass_on(step - 1, h, a).wait_recv()
            else:
                split(h, a)
            pass_on(step, h, a).start()

    to_next = pltpu.make_async_remote_copy(
        src_ref=rim_out,
        dst_ref=near_rim,
        send_sem=rim_send.at[0],
        recv_sem=rim_recv.at[0],
        device_id=ahead,
        device_id_type=MESH,
    )
    to_far = pltpu.make_async_remote_copy(
        src_ref=rim_out.at[pl.ds(1, 2)],
        dst_ref=far_rim,
        send_sem=rim_send.at[1],
        recv_sem=rim_recv.at[1],
        device_id=far_ahead,
        device_id_type=MESH,
    )

    def tap(a, j, h):
        return taps_ref[a, pl.ds(j, 1), columns(h)]

    def filtered(wide, taps_here, at):
        value = taps_here[0] * wide[pl.ds(RIM + at, chunk), :]
        for j in range(1, 3):
            value = value + taps_here[j] * wide[pl.ds(RIM + at - j, chunk), :]
        return value.astype(BF16)

    def featurize_own(h, carry):
        for a, target in enumerate((qfb.at[h], kfb.at[h], vfb.at[h])):
            base = 0 if a == 0 else past
            taps_here = [tap(a, j, h) for j in range(3)]
            wide = wide_own.at[h, a]
            wide[pl.ds(0, RIM), :] = near_rim[a, :, columns(h)].astype(F32)
            for i in range(rows // chunk):
                wide[pl.ds(RIM + i * chunk, chunk), :] = held[
                    a, pl.ds(i * chunk, chunk), columns(h)
                ].astype(F32)
                target[pl.ds(base + i * chunk, chunk), :] = filtered(wide, taps_here, i * chunk)
        return carry

    load(1).wait()
    load(2).wait()
    send_step(0, 0)
    load(0).wait()
    rim_out[...] = held[pl.ds(0, 3), pl.ds(rows - RIM, RIM), :]
    to_next.start()
    to_far.start()
    total[...] = jnp.zeros_like(total)
    for i in range(2):
        if width_of(i) < nkeys:
            blank = (pl.ds(i * tile, tile), pl.ds(width_of(i), nkeys - width_of(i)))
            for buf in (pbuf, dsbuf):
                buf[blank] = jnp.zeros((tile, nkeys - width_of(i)), BF16)
    send_step(1, 0)
    to_next.wait_recv()
    to_far.wait_recv()
    load(3).wait()
    lax.fori_loop(0, heads, featurize_own, 0)
    send_step(2, 0)
    if heads > 1:
        send_step(0, 1)

    def pass_back(step, h, a):
        return pltpu.make_async_remote_copy(
            src_ref=term_out.at[h, step, a],
            dst_ref=term_in.at[h, step, a],
            send_sem=bwd_send.at[step, h, a],
            recv_sem=bwd_recv.at[step, h, a],
            device_id=behind,
            device_id_type=MESH,
        )

    def send_back(step, h):
        for a in range(2):
            if step > 0:
                pass_back(step - 1, h, a).wait_recv()

            def piece(i, carry):
                at = pl.multiple_of(i * chunk, 16)
                here = pl.ds(at, chunk)
                term = dkv[h, a, pl.ds(step * rows + at, chunk), :]
                if step > 0:
                    term = term + decode(term_in[h, step - 1, a, here, :])
                term_out[h, step, a, here, :] = encode(term)
                return carry

            lax.fori_loop(0, rows // chunk, piece, 0)
            pass_back(step, h, a).start()

    def tail(h):
        return pltpu.make_async_remote_copy(
            src_ref=tail_out.at[h],
            dst_ref=tail_in.at[h],
            send_sem=tail_send.at[h],
            recv_sem=tail_recv.at[h],
            device_id=behind,
            device_id_type=MESH,
        )

    def settle(h, with_taps):
        last = STEPS - 1

        for a in range(2):
            pass_back(last, h, a).wait_recv()

        def piece(i, carry):
            at = pl.multiple_of(i * chunk, 16)
            here = pl.ds(at, chunk)
            dext[0, here, :] = dqb[h, here, :].astype(F32)
            for a in range(2):
                own = dkv[h, a, pl.ds(past + at, chunk), :]
                total_here = own + decode(term_in[h, last, a, here, :])
                dext[a + 1, here, :] = total_here.astype(BF16).astype(F32)
            return carry

        lax.fori_loop(0, rows // chunk, piece, 0)
        for a in range(3):
            tail_out[h, a] = dext[a, pl.ds(0, RIM), :].astype(BF16)
        tail(h).start()
        if with_taps:
            for a in range(3):
                tap_sums(h, a, wide_own.at[h, a], lambda at, n=a: dext[n, pl.ds(at, chunk), :])

    def tap_sums(h, a, wide, gradient):
        sums = [jnp.zeros((8, HEAD_DIM), F32) for _ in range(3)]
        for i in range(rows // chunk):
            value = gradient(i * chunk)
            for j in range(3):
                near = wide[pl.ds(RIM - j + i * chunk, chunk), :]
                sums[j] = sums[j] + jnp.sum((value * near).reshape(chunk // 8, 8, HEAD_DIM), axis=0)
        for j in range(3):
            here = pl.ds(3 * a + j, 1)
            total[h, here, :] = total[h, here, :] + jnp.sum(sums[j], axis=0, keepdims=True)

    def finish(h):
        tail(h).wait_recv()
        for a in range(3):
            dext[a, pl.ds(rows, RIM), :] = tail_in[h, a].astype(F32)
            taps_here = [tap(a, j, h) for j in range(3)]
            for i in range(rows // chunk):
                value = jnp.zeros((chunk, HEAD_DIM), F32)
                for j in range(3):
                    value = value + taps_here[j] * dext[a, pl.ds(i * chunk + j, chunk), :]
                (gq_ref, gk_ref, gv_ref)[a][pl.ds(i * chunk, chunk), columns(h)] = value.astype(BF16)

    def featurize(h):
        for a, target in enumerate((kfb.at[h], vfb.at[h])):
            taps_here = [tap(a + 1, j, h) for j in range(3)]
            wide = ext.at[a]
            wide[pl.ds(0, RIM), :] = far_rim[a, :, columns(h)].astype(F32)
            for i in range(past // chunk):
                here = pl.ds(i * chunk, chunk)
                wide[pl.ds(RIM + i * chunk, chunk), :] = raw[h, a, here, :].astype(F32)
                target[pl.ds(i * chunk, chunk), :] = filtered(wide, taps_here, i * chunk)

    def products(h, i):
        here = pl.ds(i * tile, tile)
        q = qfb[h, here, :]
        g = held[3, here, columns(h)]
        peak = None
        for start in range(0, width_of(i), 256):
            size = min(256, width_of(i) - start)
            part = pl.ds(start, size)
            score = dot(q, kfb[h, part, :], NT)
            if start + size > past + i * tile:
                row = lax.broadcasted_iota(jnp.int32, score.shape, 0) + i * tile
                col = lax.broadcasted_iota(jnp.int32, score.shape, 1) + (start - past)
                score = jnp.where(col <= row, score, -jnp.inf)
            sbuf[i, :, part] = score
            for n in range(0, size, HEAD_DIM):
                piece = score[:, n : n + HEAD_DIM]
                peak = piece if peak is None else jnp.maximum(peak, piece)
            dpbuf[i, :, part] = dot(g, vfb[h, part, :], NT)
        return jnp.max(peak, axis=1, keepdims=True)

    def weigh(i, peak):
        cols = pl.ds(0, width_of(i))
        stats = []
        for r in range(0, tile, strip):
            here = pl.ds(r, strip)
            weight = jnp.exp2((sbuf[i, here, cols] - peak[r : r + strip]) * exp_scale)
            sbuf[i, here, cols] = weight
            inverse = 1.0 / jnp.sum(weight, axis=1, keepdims=True)
            delta = jnp.sum(weight * dpbuf[i, here, cols], axis=1, keepdims=True) * inverse
            stats.append((inverse, delta))
        return stats

    def settle_scores(i, stats):
        cols = pl.ds(0, width_of(i))
        for n, (inverse, delta) in enumerate(stats):
            here = pl.ds(n * strip, strip)
            there = pl.ds(i * tile + n * strip, strip)
            prob = sbuf[i, here, cols] * inverse
            pbuf[there, cols] = prob.astype(BF16)
            dsbuf[there, cols] = (prob * (dpbuf[i, here, cols] - delta)).astype(BF16)

    def row_results(h, i):
        here = pl.ds(i * tile, tile)
        cols = pl.ds(0, width_of(i))
        out_ref[here, columns(h)] = dot(pbuf[here, cols], vfb[h, cols, :], NN).astype(BF16)
        dqb[h, here, :] = (dot(dsbuf[here, cols], kfb[h, cols, :], NN) * scale).astype(BF16)

    def attend_first(h):
        peak = products(h, 0)
        stats = weigh(0, peak)
        peak_next = products(h, 1)
        settle_scores(0, stats)
        stats_next = weigh(1, peak_next)
        for n, (inverse, delta) in enumerate(stats_next):
            here = pl.ds(n * strip, strip)
            norms[0, here, :] = jnp.broadcast_to(inverse, (strip, HEAD_DIM))
            norms[1, here, :] = jnp.broadcast_to(delta, (strip, HEAD_DIM))

    def attend_second(h):
        row_results(h, 0)
        stats = [
            (norms[0, pl.ds(r, strip), pl.ds(0, 1)], norms[1, pl.ds(r, strip), pl.ds(0, 1)])
            for r in range(0, tile, strip)
        ]
        settle_scores(1, stats)
        dkv[h, 1] = dot(held[3, :, columns(h)], pbuf[...], TN).T
        dkv[h, 0] = (dot(qfb[h], dsbuf[...], TN) * scale).T
        row_results(h, 1)

    def last_taps(h):
        tap_sums(h, 0, wide_own.at[h, 0], lambda at: dqb[h, pl.ds(at, chunk), :].astype(F32))
        for a in range(2):
            for block in range(BLOCKS):
                wide = wide_own.at[h, a + 1] if block == STEPS else ext.at[a, pl.ds(block * rows, RIM + rows), :]
                tap_sums(
                    h, a + 1, wide, lambda at, n=a, b=block: dkv[h, n, pl.ds(b * rows + at, chunk), :]
                )

    def head_step(h, carry):
        for a in range(2):
            pass_on(STEPS - 1, h, a).wait_recv()
        featurize(h)

        @pl.when(h < heads - 1)
        def _():
            send_step(1, h + 1)

        @pl.when(h > 1)
        def _():
            settle(h - 2, True)

        @pl.when(h > 0)
        def _():
            send_back(1, h - 1)

        attend_first(h)

        @pl.when(h < heads - 1)
        def _():
            send_step(2, h + 1)

        @pl.when(h < heads - 2)
        def _():
            send_step(0, h + 2)

        @pl.when(h > 0)
        def _():
            send_back(2, h - 1)

        @pl.when(h > 1)
        def _():
            finish(h - 2)

        attend_second(h)

        send_back(0, h)
        return carry

    lax.fori_loop(0, heads, head_step, 0)

    def sum_copy(n, m):
        group = groups[n]
        slot, device = group.other(m)
        return slot, pltpu.make_async_remote_copy(
            src_ref=slots.at[n, group.index],
            dst_ref=slots.at[n, group.index],
            send_sem=sum_send.at[n, m],
            recv_sem=sum_recv.at[n, group.index],
            device_id=device,
            device_id_type=MESH,
        )

    def sum_start(n, value):
        slots[n, groups[n].index] = value
        for m in range(1, groups[n].size):
            sum_copy(n, m)[1].start()

    def sum_end(n):
        group = groups[n]
        for m in range(1, group.size):
            slot, _ = group.other(m)
            pltpu.make_async_remote_copy(
                src_ref=slots.at[n, slot],
                dst_ref=slots.at[n, slot],
                send_sem=sum_send.at[n, m],
                recv_sem=sum_recv.at[n, slot],
                device_id=ahead,
                device_id_type=MESH,
            ).wait_recv()
        value = slots[n, 0]
        for slot in range(1, group.size):
            value = value + slots[n, slot]
        return value

    done = 0

    def sum_step():
        nonlocal done
        if done < len(groups) - 1:
            sum_start(done + 1, sum_end(done))
            done += 1

    last_taps(heads - 1)
    if heads > 1:
        settle(heads - 2, True)
    sum_start(0, total[...])
    send_back(1, heads - 1)
    if heads > 1:
        finish(heads - 2)
    sum_step()
    send_back(2, heads - 1)
    sum_step()
    settle(heads - 1, False)
    sum_step()
    finish(heads - 1)
    while done < len(groups) - 1:
        sum_step()
    value = sum_end(done)
    for h in range(heads):
        for a in range(3):
            gt_ref[a, :, columns(h)] = value[h, 3 * a : 3 * a + 3, :]

    for h in range(heads):
        tail(h).wait_send()
        for step in range(STEPS):
            for a in range(2):
                pass_on(step, h, a).wait_send()
                pass_back(step, h, a).wait_send()

    to_next.wait_send()
    to_far.wait_send()
    for n, group in enumerate(groups):
        for m in range(1, group.size):
            sum_copy(n, m)[1].wait_send()


def deliver(*refs):
    count = len(refs) // 2
    sources, targets, sems = refs[:count], refs[count : 2 * count], refs[-1]
    copies = [
        pltpu.make_async_copy(source, target, sems.at[n])
        for n, (source, target) in enumerate(zip(sources, targets, strict=True))
    ]
    for copy in copies:
        copy.start()
    for copy in copies:
        copy.wait()


def shards(n_dp, n_ctx, query_input, key_input, value_input, taps, grad_out):
    rows, width = query_input.shape[1:]
    heads = width // HEAD_DIM
    nkeys = BLOCKS * rows
    rounds = len(reduction_rounds(n_dp, n_ctx))
    members = 4 if (n_dp, n_ctx) == (8, 32) else max(n_dp, n_ctx)
    hbm = pl.BlockSpec(memory_space=pl.ANY)
    vmem = pl.BlockSpec(memory_space=pltpu.VMEM)
    flat = pltpu.VMEM((rows, width), BF16)
    dma = pltpu.SemaphoreType.DMA
    block = (rows, HEAD_DIM)
    results = pl.pallas_call(
        functools.partial(kernel, (rows, heads, n_dp, n_ctx)),
        out_shape=(flat, flat, flat, flat, pltpu.VMEM(taps.shape, F32)),
        in_specs=[hbm, hbm, hbm, vmem, hbm],
        out_specs=(vmem,) * 5,
        scratch_shapes=[
            pltpu.VMEM((4, rows, width), BF16),
            pltpu.VMEM((heads, 2, *block), BF16),
            pltpu.VMEM((3, RIM, width), BF16),
            pltpu.VMEM((3, RIM, width), BF16),
            pltpu.VMEM((2, RIM, width), BF16),
            pltpu.VMEM((heads, 2, STEPS * rows, HEAD_DIM), BF16),
            pltpu.VMEM((heads, 3, RIM + rows, HEAD_DIM), F32),
            pltpu.VMEM((2, RIM + STEPS * rows, HEAD_DIM), F32),
            pltpu.VMEM((2, rows // 2, HEAD_DIM), F32),
            pltpu.VMEM((heads, nkeys, HEAD_DIM), BF16),
            pltpu.VMEM((heads, nkeys, HEAD_DIM), BF16),
            pltpu.VMEM((heads, *block), BF16),
            pltpu.VMEM((2, rows // 2, nkeys), F32),
            pltpu.VMEM((2, rows // 2, nkeys), F32),
            pltpu.VMEM((rows, nkeys), BF16),
            pltpu.VMEM((rows, nkeys), BF16),
            pltpu.VMEM((heads, 2, nkeys, HEAD_DIM), F32),
            pltpu.VMEM((heads, *block), BF16),
            pltpu.VMEM((heads, STEPS, 2, *block), BF16),
            pltpu.VMEM((heads, STEPS, 2, *block), BF16),
            pltpu.VMEM((heads, 3, RIM, HEAD_DIM), BF16),
            pltpu.VMEM((heads, 3, RIM, HEAD_DIM), BF16),
            pltpu.VMEM((3, rows + RIM, HEAD_DIM), F32),
            pltpu.VMEM((heads, 16, HEAD_DIM), F32),
            pltpu.VMEM((rounds, members, heads, 16, HEAD_DIM), F32),
            dma((4,)),
            dma((2,)),
            dma((2,)),
            dma((STEPS, heads, 2)),
            dma((STEPS, heads, 2)),
            dma((STEPS, heads, 2)),
            dma((STEPS, heads, 2)),
            dma((heads,)),
            dma((heads,)),
            dma((rounds, members)),
            dma((rounds, members)),
        ],
        compiler_params=pltpu.CompilerParams(
            collective_id=0, has_side_effects=True, vmem_limit_bytes=52 * 1024 * 1024
        ),
    )(query_input[0], key_input[0], value_input[0], taps, grad_out[0])
    results = [pltpu.with_memory_space_constraint(result, pltpu.VMEM) for result in results]
    results = pl.pallas_call(
        deliver,
        out_shape=tuple(jax.ShapeDtypeStruct(result.shape, result.dtype) for result in results),
        in_specs=[vmem] * len(results),
        out_specs=(hbm,) * len(results),
        scratch_shapes=[dma((len(results),))],
    )(*results)
    return (*[result[None] for result in results[:4]], results[4])


def solution(mesh):
    sharded = P("dp", "ctx", "mp")
    return jax.shard_map(
        functools.partial(shards, mesh.shape["dp"], mesh.shape["ctx"]),
        mesh=mesh,
        in_specs=(sharded, sharded, sharded, P(None, None, "mp"), sharded),
        out_specs=(sharded, sharded, sharded, sharded, P(None, None, "mp")),
        check_vma=False,
    )
```
